128 devices in a mesh: outer: 16 (over y_lo, z, core), blk: 8 (over y_hi, x).
Axes of the slice: x: 4, y: 4 (y_hi: 2, y_lo: 2; y = y_hi * 2 + y_lo), z: 4, core: 2. Of those that a mesh axis runs over, the one named last changes fastest.
Arguments:
- image_feats: bfloat16 [16384, 1152], P(('outer', 'blk')), may hold values from -0.29882812 to 0.29882812
- text_feats: bfloat16 [16384, 1152], P(('outer', 'blk')), may hold values from -0.29882812 to 0.29882812
- image_weight: bfloat16 [1152, 1152], replicated, may hold values from -0.1875 to 0.1875
- text_weight: bfloat16 [1152, 1152], replicated, may hold values from -0.1875 to 0.1875
- temper: float32 [1], replicated, may hold values from 5 to 12
- offset: float32 [1], replicated, may hold values from -7 to -5
Outputs:
- image_loss: float32 [16384], P(('outer', 'blk'))
- grad_image: float32 [16384, 1152], P(('outer', 'blk'))
- grad_text: float32 [16384, 1152], P(('outer', 'blk'))
- grad_image_weight: float32 [1152, 1152], replicated
- grad_text_weight: float32 [1152, 1152], replicated
The draws below stay inside these ranges and needn't reach their ends.
All inputs are finite; a program needn't handle non-finite values.
Results may differ from the reference program's by a relative error of at most 0.017.
Values may be sent and summed in bfloat16 or wider, within the bound.
No kernel may reach another device: no remote copies, remote signals or barrier semaphores. Data moves between devices by JAX's collectives and lax.ppermute only.
A program may use at most 128 MiB of HBM per device.

```python
import math
import jax
import jax.numpy as jnp
from jax import lax

D = 1152
PAIRS = 16384


def block_scale(key, shape, pieces, smallest, high):
    level = 1.0
    for axis_at, parts in pieces:
        draws = jax.random.uniform(jax.random.fold_in(jax.random.fold_in(key, 6), axis_at), (parts,), jnp.float32, smallest / len(pieces), high / len(pieces))
        level = level * jnp.repeat(jnp.exp(draws), shape[axis_at] // parts).reshape((-1,) + (1,) * (len(shape) - 1 - axis_at))
    return level


def normal_values(rng, dims, spread, most, split=(), kind=jnp.bfloat16):
    entries = spread * jax.random.normal(rng, dims, jnp.float32)
    if split:
        entries = entries * block_scale(rng, dims, split, -0.22, 0.18)
    return jnp.clip(entries, -most, most).astype(kind)


def setup_inputs(seed: int = 0) -> dict:
    seeds = jax.random.split(jax.random.key(seed), 7)
    image_feats = normal_values(seeds[0], (PAIRS, D), 0.05, 0.29882812, ((0, 128),))
    text_feats = normal_values(seeds[1], (PAIRS, D), 0.05, 0.29882812, ((0, 128),))
    image_weight = normal_values(seeds[2], (D, D), D ** -0.5, 0.1875)
    text_weight = normal_values(seeds[3], (D, D), D ** -0.5, 0.1875)
    temper = jnp.clip(jnp.exp(jax.random.uniform(seeds[4], (1,), jnp.float32, math.log(5.0), math.log(12.0))), 5.0, 12.0)
    offset = jnp.clip(jax.random.uniform(seeds[5], (1,), jnp.float32, -7.0, -5.0), -7.0, -5.0)
    return dict(image_feats=image_feats, text_feats=text_feats, image_weight=image_weight, text_weight=text_weight, temper=temper, offset=offset)


EPS = 1e-06
HIGH = lax.Precision.HIGHEST

def tower(feats, weight):
    values = feats.astype(jnp.float32)
    centered = values - lax.optimization_barrier(jnp.mean(values, -1, keepdims=True))
    inverse = lax.rsqrt(lax.optimization_barrier(jnp.mean(centered * centered, -1, keepdims=True)) + EPS)
    normed = centered * inverse
    hidden = normed.astype(jnp.bfloat16)
    proj = jnp.dot(hidden.astype(jnp.float32), weight.astype(jnp.float32), precision=HIGH)
    scale = lax.rsqrt(lax.optimization_barrier(jnp.sum(proj * proj, -1, keepdims=True)) + EPS)
    embed = (proj * scale).astype(jnp.bfloat16)
    return (normed, inverse, hidden, proj, scale, embed)

def tower_back(state, weight, grad_embed):
    normed, inverse, hidden, proj, scale, embed = state
    grad_proj = scale * grad_embed - scale * scale * scale * proj * lax.optimization_barrier(jnp.sum(proj * grad_embed, -1, keepdims=True))
    grad_weight = jnp.dot(hidden.astype(jnp.float32).T, grad_proj, precision=HIGH)
    grad_hidden = jnp.dot(grad_proj, weight.astype(jnp.float32).T, precision=HIGH)
    centered = grad_hidden - lax.optimization_barrier(jnp.mean(grad_hidden, -1, keepdims=True))
    grad_feats = inverse * (centered - normed * lax.optimization_barrier(jnp.mean(grad_hidden * normed, -1, keepdims=True)))
    return (grad_feats, grad_weight)

def pair_terms(images, image_ids, texts, text_ids, temper, offset):
    scores = jnp.dot(images.astype(jnp.float32), texts.astype(jnp.float32).T, precision=HIGH)
    logits = temper[0] * scores + offset[0]
    signs = jnp.where(image_ids[:, None] == text_ids[None, :], 1.0, -1.0).astype(logits.dtype)
    flipped = -signs * logits
    loss_rows = lax.optimization_barrier(jnp.sum(jax.nn.softplus(flipped), 1))
    weights = (-temper[0] * signs * jax.nn.sigmoid(flipped)).astype(jnp.bfloat16)
    return (weights, loss_rows)

def reference(image_feats, text_feats, image_weight, text_weight, temper, offset):
    image_state = tower(image_feats, image_weight)
    text_state = tower(text_feats, text_weight)
    img_embed = image_state[5]
    txt_embed = text_state[5]
    block = math.gcd(512, PAIRS)
    text_ids = jnp.arange(PAIRS, dtype=jnp.int32)
    text_values = txt_embed.astype(jnp.float32)

    def visit(grad_txt, index):
        start = (index * block).astype(jnp.int32)
        images = lax.dynamic_slice_in_dim(img_embed, start, block, 0)
        image_ids = start + jnp.arange(block, dtype=jnp.int32)
        weights, loss_rows = pair_terms(images, image_ids, txt_embed, text_ids, temper, offset)
        wide = weights.astype(jnp.float32)
        grad_img = jnp.dot(wide, text_values, precision=HIGH)
        grad_txt = grad_txt + jnp.dot(wide.T, images.astype(jnp.float32), precision=HIGH)
        return (grad_txt, (grad_img, loss_rows))
    start_grad = jnp.zeros((PAIRS, D), jnp.float32)
    grad_txt, (grad_img, image_loss) = lax.scan(visit, start_grad, jnp.arange(PAIRS // block, dtype=jnp.int32))
    grad_img = grad_img.reshape(PAIRS, D)
    image_loss = image_loss.reshape(PAIRS)
    grad_image, grad_image_weight = tower_back(image_state, image_weight, grad_img)
    grad_text, grad_text_weight = tower_back(text_state, text_weight, grad_txt)
    return (image_loss, grad_image, grad_text, grad_image_weight, grad_text_weight)
```

```python
import jax
import jax.numpy as jnp
from jax import lax
from jax.sharding import Mesh, PartitionSpec as P

EPS = 1e-06
BF = jnp.bfloat16
F32 = jnp.float32
AXES = ("yl", "z", "c", "yh", "x")


def split_mesh(mesh):
    return Mesh(mesh.devices.reshape(2, 4, 2, 2, 4), AXES)


def tower(feats, weight):
    values = feats.astype(F32)
    centered = values - jnp.mean(values, -1, keepdims=True)
    inverse = lax.rsqrt(jnp.mean(centered * centered, -1, keepdims=True) + EPS)
    normed = centered * inverse
    hidden = normed.astype(BF)
    proj = jnp.dot(hidden, weight, preferred_element_type=F32)
    scale = lax.rsqrt(jnp.sum(proj * proj, -1, keepdims=True) + EPS)
    embed = (proj * scale).astype(BF)
    return (normed, inverse, hidden, proj, scale, embed)


def back_proj(state, grad_embed):
    normed, inverse, hidden, proj, scale, embed = state
    return scale * grad_embed - scale * scale * scale * proj * jnp.sum(proj * grad_embed, -1, keepdims=True)


def back_feats(state, weight, grad_proj):
    normed, inverse, hidden, proj, scale, embed = state
    grad_hidden = lax.dot_general(grad_proj, weight, (((1,), (1,)), ((), ())), preferred_element_type=F32)
    centered = grad_hidden - jnp.mean(grad_hidden, -1, keepdims=True)
    return inverse * (centered - normed * jnp.mean(grad_hidden * normed, -1, keepdims=True))


def fetch(block, axis, step):
    return lax.ppermute(block, axis, [(i, (i - step) % 4) for i in range(4)])


def give(block, axis, step):
    return lax.ppermute(block, axis, [(i, (i + step) % 4) for i in range(4)])


def swap(block, axis):
    return lax.ppermute(block, axis, [(0, 1), (1, 0)])


STEPS = (1, 3, 2)


def gather8(block, ring, pair):
    other = swap(block, pair)
    near = [block] + [fetch(block, ring, s) for s in STEPS]
    far = [other] + [fetch(other, ring, s) for s in STEPS]
    return near + far


def scatter8(parts, ring, pair):
    def ring_sum(four):
        total = four[0].astype(F32)
        for s, part in zip(STEPS, four[1:]):
            total = total + give(part, ring, s).astype(F32)
        return total

    far = swap(ring_sum(parts[4:]).astype(BF), pair)
    return ring_sum(parts[:4]) + far.astype(F32)


def reduce_weights(part):
    rows, cols = part.shape
    mine = lax.all_to_all(part.astype(BF).reshape(16, rows // 16, cols), ("z", "x"), 0, 0, tiled=True)
    mine = jnp.sum(mine.astype(F32), 0).astype(BF)
    total = mine.astype(F32)
    for s in STEPS:
        total = total + lax.ppermute(mine, ("yl", "yh"), y_pairs(s)).astype(F32)
    total = total.astype(BF)
    full = lax.all_to_all(jnp.broadcast_to(total[None], (16,) + total.shape), ("z", "x"), 0, 0, tiled=True)
    return full.reshape(rows, cols)


def y_pairs(step):
    at = lambda y: (y % 2) * 2 + y // 2
    return [(at(y), at((y + step) % 4)) for y in range(4)]


def per_device(image_feats, text_feats, image_weight, text_weight, temper, offset):
    rows = image_feats.shape[0]
    core = lax.axis_index("c")
    image_state = tower(image_feats, image_weight)
    text_state = tower(text_feats, text_weight)
    images = jnp.concatenate(gather8(image_state[5], "x", "yh"))
    texts_same = jnp.concatenate(gather8(text_state[5], "z", "yl"))
    texts = jnp.concatenate([texts_same, swap(texts_same, "c")])
    scores = lax.dot_general(images, texts, (((1,), (1,)), ((), ())), preferred_element_type=F32)
    logits = temper[0] * scores + offset[0]
    near = lax.broadcasted_iota(jnp.int32, logits.shape, 0)
    signs = jnp.where(
        (near == lax.broadcasted_iota(jnp.int32, logits.shape, 1)) & (near < rows), 1.0, -1.0
    ).astype(F32)
    flipped = -signs * logits
    loss_rows = jnp.sum(jax.nn.softplus(flipped), 1)
    weights = (-temper[0] * signs * jax.nn.sigmoid(flipped)).astype(BF)
    grad_img = jnp.dot(weights, texts, preferred_element_type=F32).astype(BF)
    grad_txt = lax.dot_general(weights, images, (((0,), (0,)), ((), ())), preferred_element_type=F32)
    half = grad_txt.shape[0] // 2
    grad_txt = (grad_txt[:half] + swap(grad_txt[half:].astype(BF), "c").astype(F32)).astype(BF)
    grad_img = scatter8(jnp.split(grad_img, 8), "x", "yh")
    grad_txt = scatter8(jnp.split(grad_txt, 8), "z", "yl")
    loss8 = lax.all_to_all(loss_rows.reshape(8, rows)[reorder()], ("yh", "x"), 0, 0, tiled=True)
    image_loss = jnp.sum(loss8, 0)
    image_gp = back_proj(image_state, grad_img).astype(BF)
    text_gp = back_proj(text_state, grad_txt).astype(BF)
    image_pack = jnp.concatenate([image_state[2], image_gp])
    text_pack = jnp.concatenate([text_state[2], text_gp])
    keep = jnp.where(core == 0, image_pack, text_pack)
    got = swap(jnp.where(core == 0, text_pack, image_pack), "c")
    hidden = jnp.concatenate([keep[:rows], got[:rows]])
    grad_proj = jnp.concatenate([keep[rows:], got[rows:]])
    part = lax.dot_general(hidden, grad_proj, (((0,), (0,)), ((), ())), preferred_element_type=F32)
    mine = reduce_weights(part)
    other = swap(mine, "c")
    grad_image_weight = jnp.where(core == 0, mine, other).astype(F32)
    grad_text_weight = jnp.where(core == 0, other, mine).astype(F32)
    grad_image = back_feats(image_state, image_weight, image_gp)
    grad_text = back_feats(text_state, text_weight, text_gp)
    return (image_loss, grad_image, grad_text, grad_image_weight, grad_text_weight)


def reorder():
    yh, x = lax.axis_index("yh"), lax.axis_index("x")
    owner = jnp.arange(8)
    step = (owner % 4 - x) % 4
    place = jnp.where(step == 2, 3, jnp.where(step == 3, 2, step))
    return (owner // 4 != yh).astype(jnp.int32) * 4 + place


def solution(mesh):
    rows = P(AXES, None)
    in_specs = (rows, rows, P(), P(), P(), P())
    out_specs = (P(AXES), rows, rows, P(), P())
    return jax.shard_map(
        per_device, mesh=split_mesh(mesh), in_specs=in_specs, out_specs=out_specs, check_vma=False
    )
```

```python
import functools

import jax
import jax.numpy as jnp
from jax import lax
from jax.experimental import pallas as pl
from jax.experimental.pallas import tpu as pltpu
from jax.sharding import Mesh, PartitionSpec as P

EPS = 1e-06
BF = jnp.bfloat16
F32 = jnp.float32
AXES = ("yl", "z", "c", "yh", "x")


def split_mesh(mesh):
    return Mesh(mesh.devices.reshape(2, 4, 2, 2, 4), AXES)


def tower(feats, weight):
    values = feats.astype(F32)
    centered = values - jnp.mean(values, -1, keepdims=True)
    inverse = lax.rsqrt(jnp.mean(centered * centered, -1, keepdims=True) + EPS)
    normed = centered * inverse
    hidden = normed.astype(BF)
    proj = jnp.dot(hidden, weight, preferred_element_type=F32)
    scale = lax.rsqrt(jnp.sum(proj * proj, -1, keepdims=True) + EPS)
    embed = (proj * scale).astype(BF)
    return (normed, inverse, hidden, proj, scale, embed)


def back_proj(state, grad_embed):
    normed, inverse, hidden, proj, scale, embed = state
    return scale * grad_embed - scale * scale * scale * proj * jnp.sum(proj * grad_embed, -1, keepdims=True)


def back_feats(state, weight, grad_proj):
    normed, inverse, hidden, proj, scale, embed = state
    grad_hidden = lax.dot_general(grad_proj, weight, (((1,), (1,)), ((), ())), preferred_element_type=F32)
    centered = grad_hidden - jnp.mean(grad_hidden, -1, keepdims=True)
    return inverse * (centered - normed * jnp.mean(grad_hidden * normed, -1, keepdims=True))


def fetch(block, axis, step):
    return lax.ppermute(block, axis, [(i, (i - step) % 4) for i in range(4)])


def give(block, axis, step):
    return lax.ppermute(block, axis, [(i, (i + step) % 4) for i in range(4)])


def swap(block, axis):
    return lax.ppermute(block, axis, [(0, 1), (1, 0)])


STEPS = (2, 1, 3)


def ring_fetch(block, ring):
    return [block] + [fetch(block, ring, s) for s in STEPS]


LOG2E = 1.4426950408889634
VMEM = pl.BlockSpec(memory_space=pltpu.VMEM)
SMEM = pl.BlockSpec(memory_space=pltpu.SMEM)
HBM = pl.BlockSpec(memory_space=pltpu.HBM)
TILE = 512
WIDE = 384
LANES = 128


def params(mib):
    return pltpu.CompilerParams(vmem_limit_bytes=mib * 2**20)


def cost(flops, mib):
    return pl.CostEstimate(flops=flops, bytes_accessed=mib * 2**20, transcendentals=0)


def in_hbm(value):
    return pltpu.with_memory_space_constraint(value, pltpu.HBM)


def load_all(pairs, sems):
    copies = [pltpu.make_async_copy(ref, into, sems.at[at]) for at, (ref, into) in enumerate(pairs)]
    for copy in copies:
        copy.start()
    for copy in copies:
        copy.wait()


def cell(scores, temper, offset):
    e = jnp.exp2(scores * (temper * LOG2E) + offset * LOG2E)
    u = 1.0 + e
    small = e * (LOG2E - e * (0.5 * LOG2E - e * (LOG2E / 3)))
    return temper * e / u, jnp.where(e < 0.01, small, jnp.log2(u))


def positive(scores, temper, offset):
    q, loss = cell(-scores, temper, -offset)
    return -q, loss


def pair_kernel(n_img, rows, *refs):
    img_refs = refs[:n_img]
    txt_refs = refs[n_img : n_img + 2]
    place_ref, temper_ref, offset_ref = refs[n_img + 2 : n_img + 5]
    q_ref, loss_ref, images, texts, out_ref, even, odd, sems = refs[n_img + 5 :]
    n_txt = texts.shape[0] // rows
    moves = [(ref, images.at[pl.ds(at * rows, rows)]) for at, ref in enumerate(img_refs)]
    for at in range(n_txt):
        start = pl.multiple_of(place_ref[at % (n_txt // 2)] * rows, rows)
        txt_ref = txt_refs[at // (n_txt // 2)]
        moves.append((txt_ref.at[pl.ds(start, rows)], texts.at[pl.ds(at * rows, rows)]))
    load_all(moves, sems)
    temper, offset = temper_ref[0], offset_ref[0]
    tiles = texts.shape[0] // TILE
    loss_ref[...] = jnp.zeros_like(loss_ref)

    def columns(tile):
        return pl.ds(pl.multiple_of(tile * TILE, TILE), TILE)

    def multiply(tile, out):
        out[...] = lax.dot_general(
            images[...], texts[columns(tile), :], (((1,), (1,)), ((), ())), preferred_element_type=F32
        )

    def finish(tile, scores):
        q, loss = cell(scores[...], temper, offset)
        q_ref[:, columns(tile)] = q.astype(BF)
        loss_ref[...] += sum(loss[:, at : at + LANES] for at in range(0, TILE, LANES))

    multiply(0, even)
    own = even[:rows, :rows]
    here = lax.broadcasted_iota(jnp.int32, (rows, rows), 0) == lax.broadcasted_iota(jnp.int32, (rows, rows), 1)
    plain_q, plain_loss = cell(own, temper, offset)
    own_q, own_loss = positive(own, temper, offset)
    own_q = jnp.where(here, own_q, plain_q).astype(BF)
    own_loss = jnp.where(here, own_loss - plain_loss, 0.0)

    def body(pair, carry):
        multiply(2 * pair + 1, odd)
        finish(2 * pair, even)
        multiply(jnp.minimum(2 * pair + 2, tiles - 1), even)
        finish(2 * pair + 1, odd)
        return carry

    lax.fori_loop(0, tiles // 2, body, 0)
    q_ref[:rows, :rows] = own_q
    loss_ref[:rows, :] += own_loss
    half = texts.shape[0] // 2
    for at in range(0, images.shape[1], WIDE):
        out_ref[:, at : at + WIDE] = lax.dot_general(
            q_ref[:, half:], images[:, at : at + WIDE], (((0,), (0,)), ((), ())), preferred_element_type=F32
        ).astype(BF)


def pair_call(images, texts, place, temper, offset):
    rows, width = images[0].shape
    m, n = len(images) * rows, 2 * texts[0].shape[0]
    return pl.pallas_call(
        functools.partial(pair_kernel, len(images), rows),
        in_specs=[HBM] * (len(images) + 2) + [SMEM] * 3,
        out_specs=[VMEM] * 5,
        out_shape=[
            pltpu.VMEM((m, n), BF),
            pltpu.VMEM((m, LANES), F32),
            pltpu.VMEM((m, width), BF),
            pltpu.VMEM((n, width), BF),
            pltpu.HBM((n // 2, width), BF),
        ],
        scratch_shapes=[pltpu.VMEM((m, TILE), F32)] * 2 + [pltpu.SemaphoreType.DMA((len(images) + n // rows,))],
        compiler_params=params(32),
        cost_estimate=cost(4 * m * n * width, 10),
        name="pair",
    )(*[in_hbm(block) for block in (*images, *texts)], place, temper, offset)


def cut_blocks(product, at, rows, out_refs, own_ref):
    columns = slice(at, at + product.shape[1])
    for place, ref in enumerate((own_ref, *out_refs)):
        for side, first in enumerate((4 * rows, 0)):
            block = product[first + place * rows : first + (place + 1) * rows]
            ref[side * rows : (side + 1) * rows, columns] = block.astype(ref.dtype)


def grad_img_kernel(rows, q_ref, texts, loss_ref, *refs):
    width = texts.shape[1]
    for at in range(0, width, WIDE):
        product = jnp.dot(q_ref[...], texts[:, at : at + WIDE], preferred_element_type=F32)
        cut_blocks(product, at, rows, refs[:3], refs[3])
    cut_blocks(loss_ref[...], width, rows, refs[:3], refs[3])


def grad_txt_kernel(rows, q_ref, images, got_ref, place_ref, out_ref, got, total, sems):
    load_all([(got_ref, got)], sems)
    width = images.shape[1]
    for at in range(0, width, WIDE):
        product = lax.dot_general(
            q_ref[:, : got.shape[0]], images[:, at : at + WIDE], (((0,), (0,)), ((), ())), preferred_element_type=F32
        )
        total[:, at : at + WIDE] = (product + got[:, at : at + WIDE].astype(F32)).astype(BF)
    blocks = got.shape[0] // rows
    moves = []
    for at in range(blocks):
        start = pl.multiple_of(place_ref[at] * rows, rows)
        moves.append((total.at[pl.ds(at * rows, rows)], out_ref.at[pl.ds(start, rows)]))
    load_all(moves, sems)


def cut_shapes(rows, width):
    return [pltpu.HBM((2 * rows, width), BF)] * 3 + [pltpu.HBM((2 * rows, width), F32)]


def grad_img_call(q, texts, loss, rows):
    width = texts.shape[1] + LANES
    return pl.pallas_call(
        functools.partial(grad_img_kernel, rows),
        in_specs=[VMEM] * 3,
        out_specs=[VMEM] * 4,
        out_shape=cut_shapes(rows, width),
        compiler_params=params(24),
        cost_estimate=cost(2 * q.shape[0] * q.shape[1] * width, 4),
        name="grad_img",
    )(q, texts, loss)


def grad_txt_call(q, images, got, place, rows):
    width = images.shape[1]
    return pl.pallas_call(
        functools.partial(grad_txt_kernel, rows),
        in_specs=[VMEM, VMEM, HBM, SMEM],
        out_specs=HBM,
        out_shape=pltpu.HBM(got.shape, BF),
        scratch_shapes=[pltpu.VMEM(got.shape, BF)] * 2 + [pltpu.SemaphoreType.DMA((got.shape[0] // rows,))],
        compiler_params=params(24),
        cost_estimate=cost(2 * got.shape[0] * q.shape[0] * width, 6),
        name="grad_txt",
    )(q, images, in_hbm(got), place)


def ring_give(parts, ring):
    return [give(part, ring, s) for s, part in zip(STEPS, parts)] + [parts[3]]


def pair_sum(parts, pair):
    rows = parts[0].shape[0] // 2
    total = sum(part.astype(F32) for part in parts)
    return total[rows:], swap(total[:rows].astype(BF), pair)


def text_places():
    yl, z = lax.axis_index("yl"), lax.axis_index("z")
    places = [(yl ^ other) * 4 + (z + s) % 4 for other in (0, 1) for s in (0,) + STEPS]
    return jnp.stack(places).astype(jnp.int32)


def gather_text(block):
    spread = jnp.broadcast_to(block[None], (8,) + block.shape)
    return lax.all_to_all(spread, ("yl", "z"), 0, 0, tiled=True).reshape(8 * block.shape[0], block.shape[1])


def reduce_weights(part):
    rows, cols = part.shape
    mine = lax.all_to_all(part.astype(BF).reshape(16, rows // 16, cols), ("z", "x"), 0, 0, tiled=True)
    mine = jnp.sum(mine.astype(F32), 0).astype(BF)
    total = mine.astype(F32)
    for s in STEPS:
        total = total + lax.ppermute(mine, ("yl", "yh"), y_pairs(s)).astype(F32)
    total = total.astype(BF)
    full = lax.all_to_all(jnp.broadcast_to(total[None], (16,) + total.shape), ("z", "x"), 0, 0, tiled=True)
    return full.reshape(rows, cols)


def y_pairs(step):
    at = lambda y: (y % 2) * 2 + y // 2
    return [(at(y), at((y + step) % 4)) for y in range(4)]


def per_device(image_feats, text_feats, image_weight, text_weight, temper, offset):
    rows = image_feats.shape[0]
    core = lax.axis_index("c")
    text_state = tower(text_feats, text_weight)
    image_state = tower(image_feats, image_weight)
    img, txt = image_state[5], text_state[5]
    far_img, txt = lax.optimization_barrier((swap(img, "yh"), txt))
    texts = gather_text(txt)
    images = ring_fetch(img, "x") + ring_fetch(far_img, "x")
    texts, images = lax.optimization_barrier((texts, images))
    texts = [texts, swap(texts, "c")]
    place = text_places()
    q, loss, images, texts, sent = pair_call(images, texts, place, temper, offset)
    got = swap(sent, "c")
    img_parts = ring_give(grad_img_call(q, texts, loss, rows), "x")
    txt_parts = grad_txt_call(q, images, got, place, rows).reshape(8, rows, -1)
    img_parts, _ = lax.optimization_barrier((img_parts, txt_parts))
    txt_parts = lax.all_to_all(txt_parts, ("yl", "z"), 0, 0, tiled=True)
    img_near, img_far = pair_sum(img_parts, "yh")
    grad_img = img_near + img_far.astype(F32)
    grad_txt = jnp.sum(txt_parts.astype(F32), 0)
    image_loss = jnp.sum(grad_img[:, img.shape[1] :], 1) * (1.0 / LOG2E)
    grad_img = grad_img[:, : img.shape[1]]
    image_gp = back_proj(image_state, grad_img).astype(BF)
    text_gp = back_proj(text_state, grad_txt).astype(BF)
    image_pack = jnp.concatenate([image_state[2], image_gp])
    text_pack = jnp.concatenate([text_state[2], text_gp])
    keep = jnp.where(core == 0, image_pack, text_pack)
    got = swap(jnp.where(core == 0, text_pack, image_pack), "c")
    hidden = jnp.concatenate([keep[:rows], got[:rows]])
    grad_proj = jnp.concatenate([keep[rows:], got[rows:]])
    part = lax.dot_general(hidden, grad_proj, (((0,), (0,)), ((), ())), preferred_element_type=F32)
    mine = reduce_weights(part)
    other = swap(mine, "c")
    grad_image_weight = jnp.where(core == 0, mine, other).astype(F32)
    grad_text_weight = jnp.where(core == 0, other, mine).astype(F32)
    grad_image = back_feats(image_state, image_weight, image_gp)
    grad_text = back_feats(text_state, text_weight, text_gp)
    return (image_loss, grad_image, grad_text, grad_image_weight, grad_text_weight)


def solution(mesh):
    rows = P(AXES, None)
    in_specs = (rows, rows, P(), P(), P(), P())
    out_specs = (P(AXES), rows, rows, P(), P())
    return jax.shard_map(
        per_device, mesh=split_mesh(mesh), in_specs=in_specs, out_specs=out_specs, check_vma=False
    )
```

```python
import functools

import jax
import jax.numpy as jnp
from jax import lax
from jax.experimental import pallas as pl
from jax.experimental.pallas import tpu as pltpu
from jax.sharding import Mesh, PartitionSpec as P

EPS = 1e-06
BF = jnp.bfloat16
F32 = jnp.float32
AXES = ("yl", "z", "c", "yh", "x")


def split_mesh(mesh):
    return Mesh(mesh.devices.reshape(2, 4, 2, 2, 4), AXES)


def tower(feats, weight):
    values = feats.astype(F32)
    centered = values - jnp.mean(values, -1, keepdims=True)
    inverse = lax.rsqrt(jnp.mean(centered * centered, -1, keepdims=True) + EPS)
    normed = centered * inverse
    hidden = normed.astype(BF)
    proj = jnp.dot(hidden, weight, preferred_element_type=F32)
    scale = lax.rsqrt(jnp.sum(proj * proj, -1, keepdims=True) + EPS)
    embed = (proj * scale).astype(BF)
    return (normed, inverse, hidden, proj, scale, embed)


def back_proj(state, grad_embed):
    normed, inverse, hidden, proj, scale, embed = state
    return scale * grad_embed - scale * scale * scale * proj * jnp.sum(proj * grad_embed, -1, keepdims=True)


def back_feats(state, weight, grad_proj):
    normed, inverse, hidden, proj, scale, embed = state
    grad_hidden = lax.dot_general(grad_proj, weight, (((1,), (1,)), ((), ())), preferred_element_type=F32)
    centered = grad_hidden - jnp.mean(grad_hidden, -1, keepdims=True)
    return inverse * (centered - normed * jnp.mean(grad_hidden * normed, -1, keepdims=True))


def fetch(block, axis, step):
    return lax.ppermute(block, axis, [(i, (i - step) % 4) for i in range(4)])


def give(block, axis, step):
    return lax.ppermute(block, axis, [(i, (i + step) % 4) for i in range(4)])


def swap(block, axis):
    return lax.ppermute(block, axis, [(0, 1), (1, 0)])


STEPS = (2, 1, 3)


def ring_fetch(block, ring):
    return [block] + [fetch(block, ring, s) for s in STEPS]


LOG2E = 1.4426950408889634
VMEM = pl.BlockSpec(memory_space=pltpu.VMEM)
SMEM = pl.BlockSpec(memory_space=pltpu.SMEM)
HBM = pl.BlockSpec(memory_space=pltpu.HBM)
TILE = 512
WIDE = 384
LANES = 128


def params(mib):
    return pltpu.CompilerParams(vmem_limit_bytes=mib * 2**20)


def cost(flops, mib):
    return pl.CostEstimate(flops=flops, bytes_accessed=mib * 2**20, transcendentals=0)


def in_hbm(value):
    return pltpu.with_memory_space_constraint(value, pltpu.HBM)


def load_all(pairs, sems):
    copies = [pltpu.make_async_copy(ref, into, sems.at[at]) for at, (ref, into) in enumerate(pairs)]
    for copy in copies:
        copy.start()
    for copy in copies:
        copy.wait()


def cell(scores, temper, offset):
    e = jnp.exp2(scores * (temper * LOG2E) + offset * LOG2E)
    u = 1.0 + e
    small = e * (LOG2E - e * (0.5 * LOG2E - e * (LOG2E / 3)))
    return temper * e / u, jnp.where(e < 0.01, small, jnp.log2(u))


def positive(scores, temper, offset):
    q, loss = cell(-scores, temper, -offset)
    return -q, loss


def pair_kernel(n_img, rows, *refs):
    img_refs = refs[:n_img]
    txt_refs = refs[n_img : n_img + 2]
    place_ref, img_place_ref, temper_ref, offset_ref = refs[n_img + 2 : n_img + 6]
    out_ref, half_ref, grad_ref, q_ref, loss_ref, images, texts, total, even, odd, sems = refs[n_img + 6 :]
    n_txt = texts.shape[0] // rows
    moves = [(ref, images.at[pl.ds(at * rows, rows)]) for at, ref in enumerate(img_refs)]
    for at in range(n_txt):
        start = pl.multiple_of(place_ref[at % (n_txt // 2)] * rows, rows)
        txt_ref = txt_refs[at // (n_txt // 2)]
        moves.append((txt_ref.at[pl.ds(start, rows)], texts.at[pl.ds(at * rows, rows)]))
    load_all(moves, sems)
    temper, offset = temper_ref[0], offset_ref[0]
    tiles = texts.shape[0] // TILE
    loss_ref[...] = jnp.zeros_like(loss_ref)

    def columns(tile):
        return pl.ds(pl.multiple_of(tile * TILE, TILE), TILE)

    def multiply(tile, out):
        out[...] = lax.dot_general(
            images[...], texts[columns(tile), :], (((1,), (1,)), ((), ())), preferred_element_type=F32
        )

    def finish(tile, scores):
        q, loss = cell(scores[...], temper, offset)
        q_ref[:, columns(tile)] = q.astype(BF)
        loss_ref[...] += sum(loss[:, at : at + LANES] for at in range(0, TILE, LANES))

    multiply(0, even)
    own = even[:rows, :rows]
    here = lax.broadcasted_iota(jnp.int32, (rows, rows), 0) == lax.broadcasted_iota(jnp.int32, (rows, rows), 1)
    plain_q, plain_loss = cell(own, temper, offset)
    own_q, own_loss = positive(own, temper, offset)
    own_q = jnp.where(here, own_q, plain_q).astype(BF)
    own_loss = jnp.where(here, own_loss - plain_loss, 0.0)

    def body(pair, carry):
        multiply(2 * pair + 1, odd)
        finish(2 * pair, even)
        multiply(jnp.minimum(2 * pair + 2, tiles - 1), even)
        finish(2 * pair + 1, odd)
        return carry

    lax.fori_loop(0, tiles // 2, body, 0)
    q_ref[:rows, :rows] = own_q
    loss_ref[:rows, :] += own_loss
    half = texts.shape[0] // 2
    keep = pltpu.make_async_copy(q_ref.at[:, pl.ds(0, half)], half_ref, sems.at[0])
    keep.start()
    for at in range(0, images.shape[1], WIDE):
        out_ref[:, at : at + WIDE] = lax.dot_general(
            q_ref[:, half:], images[:, at : at + WIDE], (((0,), (0,)), ((), ())), preferred_element_type=F32
        ).astype(BF)
    width = texts.shape[1]
    for at in range(0, width, WIDE):
        product = jnp.dot(q_ref[...], texts[:, at : at + WIDE], preferred_element_type=F32)
        total[:, at : at + WIDE] = product.astype(BF)
    total[:, width:] = loss_ref[...].astype(BF)
    keep.wait()
    moves = []
    for at in range(n_img):
        start = pl.multiple_of(img_place_ref[at] * rows, rows)
        moves.append((total.at[pl.ds(at * rows, rows)], grad_ref.at[pl.ds(start, rows)]))
    load_all(moves, sems)


def pair_call(images, texts, place, img_place, temper, offset):
    rows, width = images[0].shape
    m, n = len(images) * rows, 2 * texts[0].shape[0]
    return pl.pallas_call(
        functools.partial(pair_kernel, len(images), rows),
        in_specs=[HBM] * (len(images) + 2) + [SMEM] * 4,
        out_specs=[VMEM] + [HBM] * 2,
        out_shape=[
            pltpu.HBM((n // 2, width), BF),
            pltpu.HBM((m, n // 2), BF),
            pltpu.HBM((m, width + LANES), BF),
        ],
        scratch_shapes=[
            pltpu.VMEM((m, n), BF),
            pltpu.VMEM((m, LANES), F32),
            pltpu.VMEM((m, width), BF),
            pltpu.VMEM((n, width), BF),
            pltpu.VMEM((m, width + LANES), BF),
            pltpu.VMEM((m, TILE), F32),
            pltpu.VMEM((m, TILE), F32),
            pltpu.SemaphoreType.DMA((len(images) + n // rows,)),
        ],
        compiler_params=params(44),
        cost_estimate=cost(6 * m * n * width, 16),
        name="pair",
    )(*[in_hbm(block) for block in (*images, *texts)], place, img_place, temper, offset)


def cut_blocks(product, at, rows, out_refs, own_ref):
    columns = slice(at, at + product.shape[1])
    for place, ref in enumerate((own_ref, *out_refs)):
        for side, first in enumerate((4 * rows, 0)):
            block = product[first + place * rows : first + (place + 1) * rows]
            ref[side * rows : (side + 1) * rows, columns] = block.astype(ref.dtype)


def grad_txt_kernel(n_img, rows, q_ref, *refs):
    img_refs, got_ref, out_refs = refs[:n_img], refs[n_img], refs[n_img + 1 : n_img + 5]
    q, images, got, sems = refs[n_img + 5 :]
    moves = [(q_ref, q)] + [(ref, images.at[pl.ds(at * rows, rows)]) for at, ref in enumerate(img_refs)]
    copies = [pltpu.make_async_copy(ref, into, sems.at[at]) for at, (ref, into) in enumerate(moves + [(got_ref, got)])]
    for copy in copies:
        copy.start()
    for copy in copies[:-1]:
        copy.wait()
    width = images.shape[1]
    for at in range(0, width, WIDE):
        product = lax.dot_general(
            q[...], images[:, at : at + WIDE], (((0,), (0,)), ((), ())), preferred_element_type=F32
        )
        if at == 0:
            copies[-1].wait()
        cut_blocks(product + got[:, at : at + WIDE].astype(F32), at, rows, out_refs[:3], out_refs[3])


def cut_shapes(rows, width):
    return [pltpu.HBM((2 * rows, width), BF)] * 3 + [pltpu.HBM((2 * rows, width), F32)]


def grad_txt_call(q, images, got, rows):
    width = images[0].shape[1]
    return pl.pallas_call(
        functools.partial(grad_txt_kernel, len(images), rows),
        in_specs=[HBM] * (2 + len(images)),
        out_specs=[VMEM] * 4,
        out_shape=cut_shapes(rows, width),
        scratch_shapes=[
            pltpu.VMEM(q.shape, BF),
            pltpu.VMEM((len(images) * rows, width), BF),
            pltpu.VMEM(got.shape, BF),
            pltpu.SemaphoreType.DMA((2 + len(images),)),
        ],
        compiler_params=params(32),
        cost_estimate=cost(2 * got.shape[0] * q.shape[0] * width, 6),
        name="grad_txt",
    )(*[in_hbm(value) for value in (q, *images, got)])


def ring_give(parts, ring):
    return [give(part, ring, s) for s, part in zip(STEPS, parts)] + [parts[3]]


def pair_sum(parts, pair):
    rows = parts[0].shape[0] // 2
    total = sum(part.astype(F32) for part in parts)
    return total[rows:], swap(total[:rows].astype(BF), pair)


def text_places():
    yl, z = lax.axis_index("yl"), lax.axis_index("z")
    places = [(yl ^ other) * 4 + (z + s) % 4 for other in (0, 1) for s in (0,) + STEPS]
    return jnp.stack(places).astype(jnp.int32)


def image_places():
    yh, x = lax.axis_index("yh"), lax.axis_index("x")
    places = [(yh ^ other) * 4 + (x + s) % 4 for other in (0, 1) for s in (0,) + STEPS]
    return jnp.stack(places).astype(jnp.int32)


def gather_text(block):
    spread = jnp.broadcast_to(block[None], (8,) + block.shape)
    return lax.all_to_all(spread, ("yl", "z"), 0, 0, tiled=True).reshape(8 * block.shape[0], block.shape[1])


def reduce_weights(part):
    rows, cols = part.shape
    mine = lax.all_to_all(part.astype(BF).reshape(16, rows // 16, cols), ("z", "x"), 0, 0, tiled=True)
    mine = jnp.sum(mine.astype(F32), 0).astype(BF)
    total = mine.astype(F32)
    for s in STEPS:
        total = total + lax.ppermute(mine, ("yl", "yh"), y_pairs(s)).astype(F32)
    total = total.astype(BF)
    full = lax.all_to_all(jnp.broadcast_to(total[None], (16,) + total.shape), ("z", "x"), 0, 0, tiled=True)
    return full.reshape(rows, cols)


def y_pairs(step):
    at = lambda y: (y % 2) * 2 + y // 2
    return [(at(y), at((y + step) % 4)) for y in range(4)]


def per_device(image_feats, text_feats, image_weight, text_weight, temper, offset):
    rows = image_feats.shape[0]
    core = lax.axis_index("c")
    text_state = tower(text_feats, text_weight)
    image_state = tower(image_feats, image_weight)
    img, txt = image_state[5], text_state[5]
    far_img, txt = lax.optimization_barrier((swap(img, "yh"), txt))
    texts = gather_text(txt)
    images = ring_fetch(img, "x") + ring_fetch(far_img, "x")
    texts, images = lax.optimization_barrier((texts, images))
    texts = [texts, swap(texts, "c")]
    place = text_places()
    sent, q_half, img_parts = pair_call(images, texts, place, image_places(), temper, offset)
    got = swap(sent, "c")
    img_parts = lax.all_to_all(img_parts.reshape(8, rows, -1), ("yh", "x"), 0, 0, tiled=True)
    txt_parts = ring_give(grad_txt_call(q_half, images, got, rows), "z")
    img_parts, txt_parts = lax.optimization_barrier((img_parts, txt_parts))
    grad_img = jnp.sum(img_parts.astype(F32), 0)
    txt_near, txt_far = pair_sum(txt_parts, "yl")
    grad_txt = txt_near + txt_far.astype(F32)
    image_loss = jnp.sum(grad_img[:, img.shape[1] :], 1) * (1.0 / LOG2E)
    grad_img = grad_img[:, : img.shape[1]]
    image_gp = back_proj(image_state, grad_img).astype(BF)
    text_gp = back_proj(text_state, grad_txt).astype(BF)
    image_pack = jnp.concatenate([image_state[2], image_gp])
    text_pack = jnp.concatenate([text_state[2], text_gp])
    keep = jnp.where(core == 0, image_pack, text_pack)
    got = swap(jnp.where(core == 0, text_pack, image_pack), "c")
    hidden = jnp.concatenate([keep[:rows], got[:rows]])
    grad_proj = jnp.concatenate([keep[rows:], got[rows:]])
    part = lax.dot_general(hidden, grad_proj, (((0,), (0,)), ((), ())), preferred_element_type=F32)
    mine = reduce_weights(part)
    other = swap(mine, "c")
    grad_image_weight = jnp.where(core == 0, mine, other).astype(F32)
    grad_text_weight = jnp.where(core == 0, other, mine).astype(F32)
    grad_image = back_feats(image_state, image_weight, image_gp)
    grad_text = back_feats(text_state, text_weight, text_gp)
    return (image_loss, grad_image, grad_text, grad_image_weight, grad_text_weight)


def solution(mesh):
    rows = P(AXES, None)
    in_specs = (rows, rows, P(), P(), P(), P())
    out_specs = (P(AXES), rows, rows, P(), P())
    return jax.shard_map(
        per_device, mesh=split_mesh(mesh), in_specs=in_specs, out_specs=out_specs, check_vma=False
    )
```

```python
import functools

import jax
import jax.numpy as jnp
from jax import lax
from jax.experimental import pallas as pl
from jax.experimental.pallas import tpu as pltpu
from jax.sharding import Mesh, PartitionSpec as P

EPS = 1e-06
BF = jnp.bfloat16
F32 = jnp.float32
AXES = ("yl", "z", "c", "yh", "x")


def split_mesh(mesh):
    return Mesh(mesh.devices.reshape(2, 4, 2, 2, 4), AXES)


def tower(feats, weight):
    values = feats.astype(F32)
    centered = values - jnp.mean(values, -1, keepdims=True)
    inverse = lax.rsqrt(jnp.mean(centered * centered, -1, keepdims=True) + EPS)
    normed = centered * inverse
    hidden = normed.astype(BF)
    proj = jnp.dot(hidden, weight, preferred_element_type=F32)
    scale = lax.rsqrt(jnp.sum(proj * proj, -1, keepdims=True) + EPS)
    embed = (proj * scale).astype(BF)
    return (normed, inverse, hidden, proj, scale, embed)


def back_proj(state, grad_embed):
    normed, inverse, hidden, proj, scale, embed = state
    return scale * grad_embed - scale * scale * scale * proj * jnp.sum(proj * grad_embed, -1, keepdims=True)


def back_feats(state, weight, grad_proj):
    normed, inverse, hidden, proj, scale, embed = state
    grad_hidden = lax.dot_general(grad_proj, weight, (((1,), (1,)), ((), ())), preferred_element_type=F32)
    centered = grad_hidden - jnp.mean(grad_hidden, -1, keepdims=True)
    return inverse * (centered - normed * jnp.mean(grad_hidden * normed, -1, keepdims=True))


def fetch(block, axis, step):
    return lax.ppermute(block, axis, [(i, (i - step) % 4) for i in range(4)])


def give(block, axis, step):
    return lax.ppermute(block, axis, [(i, (i + step) % 4) for i in range(4)])


def swap(block, axis):
    return lax.ppermute(block, axis, [(0, 1), (1, 0)])


STEPS = (2, 1, 3)


def ring_fetch(block, ring):
    return [block] + [fetch(block, ring, s) for s in STEPS]


LOG2E = 1.4426950408889634
VMEM = pl.BlockSpec(memory_space=pltpu.VMEM)
SMEM = pl.BlockSpec(memory_space=pltpu.SMEM)
HBM = pl.BlockSpec(memory_space=pltpu.HBM)
TILE = 512
WIDE = 384
LANES = 128


def params(mib):
    return pltpu.CompilerParams(vmem_limit_bytes=mib * 2**20)


def cost(flops, mib):
    return pl.CostEstimate(flops=flops, bytes_accessed=mib * 2**20, transcendentals=0)


def in_hbm(value):
    return pltpu.with_memory_space_constraint(value, pltpu.HBM)


def load_all(pairs, sems):
    copies = [pltpu.make_async_copy(ref, into, sems.at[at]) for at, (ref, into) in enumerate(pairs)]
    for copy in copies:
        copy.start()
    for copy in copies:
        copy.wait()


def cell(scores, temper, offset):
    e = jnp.exp2(scores * (temper * LOG2E) + offset * LOG2E)
    u = 1.0 + e
    small = e * (LOG2E - e * (0.5 * LOG2E - e * (LOG2E / 3)))
    return temper * e / u, jnp.where(e < 0.01, small, jnp.log2(u))


def positive(scores, temper, offset):
    q, loss = cell(-scores, temper, -offset)
    return -q, loss


def pair_kernel(n_img, rows, *refs):
    img_refs = refs[:n_img]
    txt_refs = refs[n_img : n_img + 2]
    place_ref, img_place_ref, temper_ref, offset_ref = refs[n_img + 2 : n_img + 6]
    out_ref, half_ref, grad_ref, q_ref, loss_ref, images, texts, total, even, odd, sems = refs[n_img + 6 :]
    n_txt = texts.shape[0] // rows
    moves = [(ref, images.at[pl.ds(at * rows, rows)]) for at, ref in enumerate(img_refs)]
    for at in range(n_txt):
        start = pl.multiple_of(place_ref[at % (n_txt // 2)] * rows, rows)
        txt_ref = txt_refs[at // (n_txt // 2)]
        moves.append((txt_ref.at[pl.ds(start, rows)], texts.at[pl.ds(at * rows, rows)]))
    load_all(moves, sems)
    temper, offset = temper_ref[0], offset_ref[0]
    tiles = texts.shape[0] // TILE
    loss_ref[...] = jnp.zeros_like(loss_ref)

    def columns(tile):
        return pl.ds(tile * TILE, TILE)

    def multiply(tile, out):
        out[...] = lax.dot_general(
            images[...], texts[columns(tile), :], (((1,), (1,)), ((), ())), preferred_element_type=F32
        )

    def finish(tile, scores):
        q, loss = cell(scores[...], temper, offset)
        q_ref[:, columns(tile)] = q.astype(BF)
        loss_ref[...] += sum(loss[:, at : at + LANES] for at in range(0, TILE, LANES))

    multiply(0, even)
    own = even[:rows, :rows]
    here = lax.broadcasted_iota(jnp.int32, (rows, rows), 0) == lax.broadcasted_iota(jnp.int32, (rows, rows), 1)
    plain_q, plain_loss = cell(own, temper, offset)
    own_q, own_loss = positive(own, temper, offset)
    own_q = jnp.where(here, own_q, plain_q).astype(BF)
    own_loss = jnp.where(here, own_loss - plain_loss, 0.0)

    buffers = (even, odd)
    for tile in range(tiles):
        if tile + 1 < tiles:
            multiply(tile + 1, buffers[(tile + 1) % 2])
        finish(tile, buffers[tile % 2])
    q_ref[:rows, :rows] = own_q
    loss_ref[:rows, :] += own_loss
    half = texts.shape[0] // 2
    keep = pltpu.make_async_copy(q_ref.at[:, pl.ds(0, half)], half_ref, sems.at[0])
    keep.start()
    for at in range(0, images.shape[1], WIDE):
        out_ref[:, at : at + WIDE] = lax.dot_general(
            q_ref[:, half:], images[:, at : at + WIDE], (((0,), (0,)), ((), ())), preferred_element_type=F32
        ).astype(BF)
    width = texts.shape[1]
    for at in range(0, width, WIDE):
        product = jnp.dot(q_ref[...], texts[:, at : at + WIDE], preferred_element_type=F32)
        total[:, at : at + WIDE] = product.astype(BF)
    total[:, width:] = loss_ref[...].astype(BF)
    keep.wait()
    moves = []
    for at in range(n_img):
        start = pl.multiple_of(img_place_ref[at] * rows, rows)
        moves.append((total.at[pl.ds(at * rows, rows)], grad_ref.at[pl.ds(start, rows)]))
    load_all(moves, sems)


def pair_call(images, texts, place, img_place, temper, offset):
    rows, width = images[0].shape
    m, n = len(images) * rows, 2 * texts[0].shape[0]
    return pl.pallas_call(
        functools.partial(pair_kernel, len(images), rows),
        in_specs=[HBM] * (len(images) + 2) + [SMEM] * 4,
        out_specs=[VMEM] + [HBM] * 2,
        out_shape=[
            pltpu.HBM((n // 2, width), BF),
            pltpu.HBM((m, n // 2), BF),
            pltpu.HBM((m, width + LANES), BF),
        ],
        scratch_shapes=[
            pltpu.VMEM((m, n), BF),
            pltpu.VMEM((m, LANES), F32),
            pltpu.VMEM((m, width), BF),
            pltpu.VMEM((n, width), BF),
            pltpu.VMEM((m, width + LANES), BF),
            pltpu.VMEM((m, TILE), F32),
            pltpu.VMEM((m, TILE), F32),
            pltpu.SemaphoreType.DMA((len(images) + n // rows,)),
        ],
        compiler_params=params(44),
        cost_estimate=cost(6 * m * n * width, 16),
        name="pair",
    )(*[in_hbm(block) for block in (*images, *texts)], place, img_place, temper, offset)


def cut_blocks(product, at, rows, out_refs, own_ref):
    columns = slice(at, at + product.shape[1])
    for place, ref in enumerate((own_ref, *out_refs)):
        for side, first in enumerate((4 * rows, 0)):
            block = product[first + place * rows : first + (place + 1) * rows]
            ref[side * rows : (side + 1) * rows, columns] = block.astype(ref.dtype)


def grad_txt_kernel(n_img, rows, q_ref, *refs):
    img_refs, got_ref, out_refs = refs[:n_img], refs[n_img], refs[n_img + 1 : n_img + 5]
    q, images, got, sems = refs[n_img + 5 :]
    moves = [(q_ref, q)] + [(ref, images.at[pl.ds(at * rows, rows)]) for at, ref in enumerate(img_refs)]
    copies = [pltpu.make_async_copy(ref, into, sems.at[at]) for at, (ref, into) in enumerate(moves + [(got_ref, got)])]
    for copy in copies:
        copy.start()
    for copy in copies[:-1]:
        copy.wait()
    width = images.shape[1]
    for at in range(0, width, WIDE):
        product = lax.dot_general(
            q[...], images[:, at : at + WIDE], (((0,), (0,)), ((), ())), preferred_element_type=F32
        )
        if at == 0:
            copies[-1].wait()
        cut_blocks(product + got[:, at : at + WIDE].astype(F32), at, rows, out_refs[:3], out_refs[3])


def cut_shapes(rows, width):
    return [pltpu.HBM((2 * rows, width), BF)] * 3 + [pltpu.HBM((2 * rows, width), F32)]


def grad_txt_call(q, images, got, rows):
    width = images[0].shape[1]
    return pl.pallas_call(
        functools.partial(grad_txt_kernel, len(images), rows),
        in_specs=[HBM] * (2 + len(images)),
        out_specs=[VMEM] * 4,
        out_shape=cut_shapes(rows, width),
        scratch_shapes=[
            pltpu.VMEM(q.shape, BF),
            pltpu.VMEM((len(images) * rows, width), BF),
            pltpu.VMEM(got.shape, BF),
            pltpu.SemaphoreType.DMA((2 + len(images),)),
        ],
        compiler_params=params(32),
        cost_estimate=cost(2 * got.shape[0] * q.shape[0] * width, 6),
        name="grad_txt",
    )(*[in_hbm(value) for value in (q, *images, got)])


def ring_give(parts, ring):
    return [give(part, ring, s) for s, part in zip(STEPS, parts)] + [parts[3]]


def pair_sum(parts, pair):
    rows = parts[0].shape[0] // 2
    total = sum(part.astype(F32) for part in parts)
    return total[rows:], swap(total[:rows].astype(BF), pair)


def text_places():
    yl, z = lax.axis_index("yl"), lax.axis_index("z")
    places = [(yl ^ other) * 4 + (z + s) % 4 for other in (0, 1) for s in (0,) + STEPS]
    return jnp.stack(places).astype(jnp.int32)


def image_places():
    yh, x = lax.axis_index("yh"), lax.axis_index("x")
    places = [(yh ^ other) * 4 + (x + s) % 4 for other in (0, 1) for s in (0,) + STEPS]
    return jnp.stack(places).astype(jnp.int32)


def gather_text(block):
    spread = jnp.broadcast_to(block[None], (8,) + block.shape)
    return lax.all_to_all(spread, ("yl", "z"), 0, 0, tiled=True).reshape(8 * block.shape[0], block.shape[1])


def reduce_weights(part):
    rows, cols = part.shape
    mine = lax.all_to_all(part.astype(BF).reshape(16, rows // 16, cols), ("z", "x"), 0, 0, tiled=True)
    mine = jnp.sum(mine.astype(F32), 0).astype(BF)
    total = mine.astype(F32)
    for s in STEPS:
        total = total + lax.ppermute(mine, ("yl", "yh"), y_pairs(s)).astype(F32)
    total = total.astype(BF)
    full = lax.all_to_all(jnp.broadcast_to(total[None], (16,) + total.shape), ("z", "x"), 0, 0, tiled=True)
    return full.reshape(rows, cols)


def y_pairs(step):
    at = lambda y: (y % 2) * 2 + y // 2
    return [(at(y), at((y + step) % 4)) for y in range(4)]


def per_device(image_feats, text_feats, image_weight, text_weight, temper, offset):
    rows = image_feats.shape[0]
    core = lax.axis_index("c")
    text_state = tower(text_feats, text_weight)
    image_state = tower(image_feats, image_weight)
    img, txt = image_state[5], text_state[5]
    far_img, txt = lax.optimization_barrier((swap(img, "yh"), txt))
    texts = gather_text(txt)
    images = ring_fetch(img, "x") + ring_fetch(far_img, "x")
    texts, images = lax.optimization_barrier((texts, images))
    texts = [texts, swap(texts, "c")]
    place = text_places()
    sent, q_half, img_parts = pair_call(images, texts, place, image_places(), temper, offset)
    got = swap(sent, "c")
    img_parts = lax.all_to_all(img_parts.reshape(8, rows, -1), ("yh", "x"), 0, 0, tiled=True)
    txt_parts = ring_give(grad_txt_call(q_half, images, got, rows), "z")
    img_parts, txt_parts = lax.optimization_barrier((img_parts, txt_parts))
    grad_img = jnp.sum(img_parts.astype(F32), 0)
    txt_near, txt_far = pair_sum(txt_parts, "yl")
    grad_txt = txt_near + txt_far.astype(F32)
    image_loss = jnp.sum(grad_img[:, img.shape[1] :], 1) * (1.0 / LOG2E)
    grad_img = grad_img[:, : img.shape[1]]
    image_gp = back_proj(image_state, grad_img).astype(BF)
    text_gp = back_proj(text_state, grad_txt).astype(BF)
    image_pack = jnp.concatenate([image_state[2], image_gp])
    text_pack = jnp.concatenate([text_state[2], text_gp])
    keep = jnp.where(core == 0, image_pack, text_pack)
    got = swap(jnp.where(core == 0, text_pack, image_pack), "c")
    hidden = jnp.concatenate([keep[:rows], got[:rows]])
    grad_proj = jnp.concatenate([keep[rows:], got[rows:]])
    part = lax.dot_general(hidden, grad_proj, (((0,), (0,)), ((), ())), preferred_element_type=F32)
    mine = reduce_weights(part)
    other = swap(mine, "c")
    grad_image_weight = jnp.where(core == 0, mine, other).astype(F32)
    grad_text_weight = jnp.where(core == 0, other, mine).astype(F32)
    grad_image = back_feats(image_state, image_weight, image_gp)
    grad_text = back_feats(text_state, text_weight, text_gp)
    return (image_loss, grad_image, grad_text, grad_image_weight, grad_text_weight)


def solution(mesh):
    rows = P(AXES, None)
    in_specs = (rows, rows, P(), P(), P(), P())
    out_specs = (P(AXES), rows, rows, P(), P())
    return jax.shard_map(
        per_device, mesh=split_mesh(mesh), in_specs=in_specs, out_specs=out_specs, check_vma=False
    )
```
